32 devices in a mesh: cmp: 4 (over x, core), lmk: 8 (over z, y).
Axes of the slice: x: 2, y: 2, z: 4, core: 2. Of those that a mesh axis runs over, the one named last changes fastest.
Arguments:
- compounds: bfloat16 [32768, 512], P(('cmp', 'lmk')), may hold values from -6 to 6
- targets: bfloat16 [32768, 128], P(('cmp', 'lmk')), may hold values from -6 to 6
- cluster_lists: int32 [32768, 4], P(('cmp', 'lmk')), may hold values from 0 to 127, as said below
- landmarks: bfloat16 [128, 256, 512], P('lmk'), may hold values from -6 to 6
- neighbours: int32 [128, 8], replicated, may hold values from 0 to 127, as said below
Outputs:
- normal_blocks: float32 [256, 128, 8, 256], P('cmp', 'lmk')
- right_sides: float32 [256, 128, 128], P('cmp', 'lmk')
The draws below stay inside these ranges and needn't reach their ends.
Inputs may be any that keep to these rules, and one draw needn't show every extreme that they name: `cluster_lists`: each compound lists 4 different clusters, each within 7 clusters of its first entry, counted cyclically modulo 128. In each aligned block of 1024 rows (the compounds of one device) no cluster is listed by more than 64 rows, and in every block some cluster is listed by exactly 64. neighbours[a, 0] = a; the entries of a row are distinct; every row has the same offsets, neighbours[a, j] = (a + neighbours[0, j]) modulo 128, and each entry differs from a by at most 8 clusters, counted cyclically.
All inputs are finite; a program needn't handle non-finite values.
Results may differ from the reference program's by a relative error of at most 0.0048.
Values may be sent and summed in bfloat16 or wider, within the bound.
A program may use at most 192 MiB of HBM per device.

```python
import math
import jax
import jax.numpy as jnp
from jax import lax

E = 512
M = 256
Q = 128
NBR = 8
PICKS = 4
CL_DEV = 16
CMP_DEV = 1024
CLUSTERS = 128
NCMP = 32768
PMAX = 16
CAP = 64
N_CMP = 4
N_LMK = 8


def neighbour_offsets(key):
    sub_key = jax.random.fold_in(key, 7)
    rim_width = CL_DEV // 2
    distances = jnp.arange(1, rim_width + 1, dtype=jnp.int32)
    below_side = -jax.random.permutation(jax.random.fold_in(sub_key, 1), distances)
    above_side = jax.random.permutation(jax.random.fold_in(sub_key, 2), distances)
    remaining = jax.random.permutation(jax.random.fold_in(sub_key, 3), jnp.concatenate([below_side[1:], above_side[1:]]))[:NBR - 3]
    picked = jnp.concatenate([below_side[:1], above_side[:1], remaining]).astype(jnp.int32)
    picked = jax.random.permutation(jax.random.fold_in(sub_key, 4), picked)
    return jnp.concatenate([jnp.zeros((1,), jnp.int32), picked]).astype(jnp.int32)


def draw_neighbours(key, part):
    offsets = neighbour_offsets(key)
    clusters = jnp.arange(CLUSTERS, dtype=jnp.int32)
    return jnp.mod(clusters[:, None] + offsets[None, :], CLUSTERS).astype(jnp.int32)


def draw_cluster_lists(key, part):
    hot_cluster = jax.random.randint(jax.random.fold_in(key, 11), (), 0, CLUSTERS).astype(jnp.int32)
    slot_ids = jnp.arange(CLUSTERS * PMAX, dtype=jnp.int32)
    slot_cluster = slot_ids // PMAX
    slot_window = slot_cluster // 2
    spans = jnp.concatenate([jnp.arange(-(PICKS - 1), 0), jnp.arange(1, PICKS)]).astype(jnp.int32)

    def one_block(block_key):
        sign_bit = jax.random.randint(jax.random.fold_in(block_key, 1), (), 0, 2).astype(jnp.int32)
        widest = (2 * sign_bit - 1) * (PICKS - 1)
        span_scores = jax.random.randint(jax.random.fold_in(block_key, 2), (spans.shape[0],), 0, 1 << 20)
        span_scores = jnp.where(spans == widest, 1 << 21, span_scores)
        others = spans[jnp.argsort(span_scores, stable=True)[:PICKS - 2]]
        shifts = 2 * jnp.concatenate([widest[None], others]).astype(jnp.int32)
        forced_windows = jnp.concatenate([hot_cluster[None], jnp.mod(hot_cluster - shifts, CLUSTERS)]) // 2
        forced = jnp.any(slot_window[:, None] == forced_windows[None, :], axis=1)
        scores = jax.random.randint(block_key, (CLUSTERS * PMAX,), 0, 1 << 20)
        scores = jnp.where(forced, -1, scores)
        chosen = jnp.argsort(scores, stable=True)[:CMP_DEV].astype(jnp.int32)
        columns = [chosen // PMAX]
        for pick in range(PICKS - 1):
            jitter = jax.random.randint(jax.random.fold_in(block_key, 20 + pick), (CLUSTERS * PMAX,), 0, 1 << 16)
            within = jnp.argsort(slot_window * (1 << 17) + jitter, stable=True).astype(jnp.int32)
            columns.append(jnp.mod(within[chosen] // PMAX + shifts[pick], CLUSTERS))
        listing = jnp.stack(columns, axis=1).astype(jnp.int32)
        return jax.random.permutation(jax.random.fold_in(block_key, 3), listing, axis=0)
    block_keys = jax.vmap(lambda index: jax.random.fold_in(jax.random.fold_in(key, 13), index))(jnp.arange(N_CMP * N_LMK))
    return jax.vmap(one_block)(block_keys).reshape(NCMP, PICKS).astype(jnp.int32)


def block_levels(stream_key, dims, pieces, least, high):
    loudness, own = 1.0, jax.random.fold_in(stream_key, 6)
    for position, shards_of in pieces:
        draws = jnp.exp(jax.random.uniform(jax.random.fold_in(own, position), (shards_of,), jnp.float32, least / len(pieces), high / len(pieces)))
        loudness = loudness * jnp.repeat(draws, dims[position] // shards_of).reshape([-1 if axis == position else 1 for axis in range(len(dims))])
    return loudness


def gaussian(own_key, extent, scale, reach, shards=(), held_as=jnp.bfloat16):
    loudness = block_levels(own_key, extent, shards, -0.22, 0.18) if shards else 1.0
    drawn = jax.random.normal(own_key, extent, jnp.float32) * scale * loudness
    return jnp.minimum(jnp.maximum(drawn, -reach), reach).astype(held_as)


def setup_inputs(seed: int = 0) -> dict:
    arg_keys = jax.random.split(jax.random.key(seed), 6)
    compounds = gaussian(arg_keys[0], (NCMP, E), 1.0, 6.0, ((0, 32),))
    targets = gaussian(arg_keys[1], (NCMP, Q), 1.0, 6.0, ((0, 32),))
    cluster_lists = draw_cluster_lists(jax.random.fold_in(arg_keys[5], 71), 0)
    landmarks = gaussian(arg_keys[3], (CLUSTERS, M, E), 1.0, 6.0, ((0, 8),))
    neighbours = draw_neighbours(jax.random.fold_in(arg_keys[5], 71), 0)
    return dict(compounds=compounds, targets=targets, cluster_lists=cluster_lists, landmarks=landmarks, neighbours=neighbours)


def normalize(data):
    wide = data.astype(jnp.float32)
    return (wide * lax.rsqrt(lax.optimization_barrier(jnp.sum(wide * wide, axis=-1, keepdims=True)) + 1e-06)).astype(jnp.bfloat16)

def reference(compounds, targets, cluster_lists, landmarks, neighbours):
    unit_rows = normalize(compounds)
    unit_marks = normalize(landmarks)
    flat_lists = cluster_lists.reshape(-1)
    slot_count = N_CMP * N_LMK * CAP
    kernel_scale = 0.75 * math.sqrt(E)

    def one_cluster(cluster):
        hits = flat_lists == cluster
        found = jnp.nonzero(hits, size=slot_count, fill_value=0)[0].astype(jnp.int32)
        live = jnp.arange(slot_count, dtype=jnp.int32) < jnp.sum(hits.astype(jnp.int32))
        owner = found // PICKS
        rows = unit_rows[owner]
        aims = targets[owner]
        listed = cluster_lists[owner]
        near = neighbours[cluster]
        flags = jnp.any(near[None, :, None] == listed[:, None, :], axis=2) & live[:, None]
        marks = unit_marks[near].reshape(NBR * M, E)
        scores = jnp.dot(rows, marks.T, preferred_element_type=jnp.float32)
        kern = jnp.exp(kernel_scale * scores - 4.0) * jnp.repeat(flags.astype(jnp.float32), M, axis=1)
        kern = kern.astype(jnp.bfloat16)
        tiles = jnp.concatenate([kern, aims], axis=1)
        return jnp.dot(kern[:, :M].T, tiles, preferred_element_type=jnp.float32)
    blocks = lax.map(one_cluster, jnp.arange(CLUSTERS, dtype=jnp.int32))
    blocks = jnp.transpose(blocks, (1, 0, 2))
    normal_blocks = blocks[:, :, :NBR * M].reshape(M, CLUSTERS, NBR, M)
    right_sides = blocks[:, :, NBR * M:]
    return (normal_blocks, right_sides)
```

```python
import functools
import math

import jax
import jax.numpy as jnp
from jax import lax
from jax.experimental import pallas as pl
from jax.experimental.pallas import tpu as pltpu
from jax.sharding import PartitionSpec as P

LIFT = 8.0
FLAG_LANES = 128
CHUNKS = 4


def normalize(data):
    wide = data.astype(jnp.float32)
    return (wide * lax.rsqrt(jnp.sum(wide * wide, axis=-1, keepdims=True) + 1e-06)).astype(
        jnp.bfloat16
    )


def dispatch_kernel(
    cluster_count, first_ref, lists_ref, rows_ref, out_ref, rank_ref, hit_ref
):
    sources, picks, count = lists_ref.shape
    owned, _, cap, _ = out_ref.shape
    width = rows_ref.shape[2] - FLAG_LANES
    rim = owned // 2
    extended = owned + 2 * rim
    step = pl.program_id(0)

    @pl.when(step == 0)
    def _():
        first = first_ref[0]
        index = lax.broadcasted_iota(jnp.int32, (FLAG_LANES, count), 0)
        ident = index + (first - rim + cluster_count)
        ident = jnp.where(ident >= cluster_count, ident - cluster_count, ident)
        ident = jnp.where(ident >= cluster_count, ident - cluster_count, ident)
        ident = jnp.where(index < extended, ident, -1)
        for source in range(sources):
            hit = lists_ref[source, 0:1, :] == ident
            for pick in range(1, picks):
                hit = hit | (lists_ref[source, pick : pick + 1, :] == ident)
            hit_ref[source] = jnp.where(hit, 1.0, 0.0).astype(jnp.bfloat16)
        before = lax.broadcasted_iota(jnp.int32, (count, count), 0) < lax.broadcasted_iota(
            jnp.int32, (count, count), 1
        )
        before = jnp.where(before, 1.0, 0.0).astype(jnp.bfloat16)
        own = hit_ref[:, rim : rim + owned, :].reshape(sources * owned, count)
        rank = jnp.dot(own, before, preferred_element_type=jnp.float32)
        rank = jnp.where(own.astype(jnp.float32) > 0.5, rank, -1.0)
        rank_ref[...] = rank.astype(jnp.int32).reshape(sources, owned, count)

    group = max(1, 256 // cap)
    slot = lax.broadcasted_iota(jnp.int32, (cap, count), 0)
    for start in range(0, owned, group):
        picked = jnp.concatenate(
            [
                jnp.where(rank_ref[step, pl.ds(start + k, 1), :] == slot, 1.0, 0.0).astype(
                    jnp.bfloat16
                )
                for k in range(group)
            ],
            axis=0,
        )
        moved = jnp.dot(picked, rows_ref[0], preferred_element_type=jnp.float32)
        flags = lax.dot_general(
            picked, hit_ref[step], (((1,), (1,)), ((), ())), preferred_element_type=jnp.float32
        )
        moved = moved.astype(jnp.bfloat16).reshape(group, cap, moved.shape[1])
        flags = flags.astype(jnp.bfloat16).reshape(group, cap, FLAG_LANES)
        out_ref[start : start + group, 0, :, :width] = moved[:, :, :width]
        out_ref[start : start + group, 0, :, width : width + FLAG_LANES] = flags
        out_ref[start : start + group, 0, :, width + FLAG_LANES :] = moved[:, :, width:]


def dispatch(first, lists, rows, owned, cap, cluster_count):
    sources, picks, count = lists.shape
    total = rows.shape[2] + FLAG_LANES
    return pl.pallas_call(
        functools.partial(dispatch_kernel, cluster_count),
        grid=(sources,),
        in_specs=[
            pl.BlockSpec(memory_space=pltpu.SMEM),
            pl.BlockSpec((sources, picks, count), lambda s: (0, 0, 0)),
            pl.BlockSpec((1, count, rows.shape[2]), lambda s: (s, 0, 0)),
        ],
        out_specs=pl.BlockSpec((owned, 1, cap, total), lambda s: (0, s, 0, 0)),
        out_shape=jax.ShapeDtypeStruct((owned, sources, cap, total), jnp.bfloat16),
        scratch_shapes=[
            pltpu.VMEM((sources, owned, count), jnp.int32),
            pltpu.VMEM((sources, FLAG_LANES, count), jnp.bfloat16),
        ],
        compiler_params=pltpu.CompilerParams(vmem_limit_bytes=48 * 2**20),
        cost_estimate=pl.CostEstimate(
            flops=2 * sources * owned * cap * count * total,
            bytes_accessed=2 * sources * (count * rows.shape[2] + owned * cap * total),
            transcendentals=0,
        ),
    )(first, lists, rows)


def block_kernel(base, near_count, scale, spots_ref, slots_ref, marks_ref, keep_ref, send_ref):
    mark_count = marks_ref.shape[1]
    depth = marks_ref.shape[2]
    parts, rows = keep_ref.shape[1], keep_ref.shape[2]
    cluster = base + pl.program_id(0)
    odd = spots_ref[spots_ref.shape[0] - 1] == 1
    factor = scale * math.log2(math.e)
    shift = LIFT * factor + 4.0 * math.log2(math.e)
    left = slots_ref[0, :, :depth]

    def kern(near_slot):
        marks = marks_ref[spots_ref[cluster * near_count + near_slot]]
        scores = lax.dot_general(
            left, marks, (((1,), (1,)), ((), ())), preferred_element_type=jnp.float32
        )
        return jnp.exp2(scores * factor - shift).astype(jnp.bfloat16)

    def store(block, column):
        width = block.shape[1]
        for part in range(parts):
            low = block[2 * part * rows : (2 * part + 1) * rows]
            high = block[(2 * part + 1) * rows : (2 * part + 2) * rows]
            keep_ref[0, part, :, column : column + width] = jnp.where(odd, high, low).astype(
                jnp.bfloat16
            )
            send_ref[0, part, :, column : column + width] = jnp.where(odd, low, high).astype(
                jnp.bfloat16
            )

    own = kern(0)
    turned = own.T
    for near_slot in range(near_count):
        other = own if near_slot == 0 else kern(near_slot)
        store(
            jnp.dot(turned, other, preferred_element_type=jnp.float32), near_slot * mark_count
        )
    store(
        jnp.dot(turned, slots_ref[0, :, depth:], preferred_element_type=jnp.float32),
        near_count * mark_count,
    )


def blocks(base, clusters, near_count, scale, parts, spots, slots, marks):
    mark_count, depth = marks.shape[1], marks.shape[2]
    slot_count = slots.shape[1]
    width = near_count * mark_count + slots.shape[2] - depth
    rows = mark_count // (2 * parts)
    shape = jax.ShapeDtypeStruct((clusters, parts, rows, width), jnp.bfloat16)
    spec = pl.BlockSpec((1, parts, rows, width), lambda a: (a, 0, 0, 0))
    return pl.pallas_call(
        functools.partial(block_kernel, base, near_count, scale),
        grid=(clusters,),
        in_specs=[
            pl.BlockSpec(memory_space=pltpu.SMEM),
            pl.BlockSpec((1, slot_count, slots.shape[2]), lambda a: (a + base, 0, 0)),
            pl.BlockSpec(marks.shape, lambda a: (0, 0, 0), pipeline_mode=pl.Buffered(1)),
        ],
        out_specs=[spec, spec],
        out_shape=[shape, shape],
        compiler_params=pltpu.CompilerParams(vmem_limit_bytes=48 * 2**20),
        cost_estimate=pl.CostEstimate(
            flops=2 * clusters * slot_count * width * (depth + mark_count),
            bytes_accessed=2 * marks.size + 2 * clusters * (slot_count * 768 + 256 * width),
            transcendentals=clusters * slot_count * width,
        ),
    )(spots, slots, marks)


def on_device(compounds, targets, cluster_lists, landmarks, neighbours):
    lmk_count = lax.axis_size("lmk")
    cmp_count = lax.axis_size("cmp")
    my_lmk = lax.axis_index("lmk")
    my_cmp = lax.axis_index("cmp")
    owned, mark_count, width = landmarks.shape
    rim = owned // 2
    near_count = neighbours.shape[1]
    cluster_count = neighbours.shape[0]
    cap = cluster_lists.shape[1] * (2 * compounds.shape[0] // cluster_count)
    scale = 0.75 * math.sqrt(width)
    first = my_lmk * owned

    rows = jnp.concatenate([normalize(compounds), targets], axis=1)
    all_rows = lax.all_gather(rows, "lmk")
    all_lists = lax.all_gather(cluster_lists.T, "lmk")

    forward = [(i, (i + 1) % lmk_count) for i in range(lmk_count)]
    backward = [(target, source) for source, target in forward]
    unit_marks = normalize(landmarks)
    low = lax.ppermute(unit_marks[owned - rim :], "lmk", forward)
    high = lax.ppermute(unit_marks[:rim], "lmk", backward)
    extended = jnp.concatenate([low, unit_marks, high], axis=0)
    lift = jnp.where(
        jnp.arange(owned + 2 * rim)[:, None, None] == jnp.arange(FLAG_LANES)[None, None, :],
        LIFT,
        0.0,
    ).astype(jnp.bfloat16)
    lift = jnp.broadcast_to(lift, (owned + 2 * rim, mark_count, FLAG_LANES))
    extended = jnp.concatenate([extended, lift], axis=2)

    near = lax.dynamic_slice_in_dim(neighbours, first, owned, 0)
    spots = jnp.mod(near - first + rim, cluster_count).reshape(-1)
    my_core = my_cmp % 2
    my_part = my_cmp // 2
    spots = jnp.concatenate([spots, my_core[None]]).astype(jnp.int32)

    slots = dispatch(
        jnp.asarray(first, jnp.int32)[None], all_lists, all_rows, owned, cap, cluster_count
    )
    slots = slots.reshape(owned, lmk_count * cap, slots.shape[3])
    parts = cmp_count // 2
    cores = [(i, i ^ 1) for i in range(cmp_count)]
    each = owned // CHUNKS
    done = []
    for chunk in range(CHUNKS):
        keep, send = blocks(
            chunk * each, each, near_count, scale, parts, spots, slots, extended
        )
        got = lax.ppermute(send, "cmp", cores)
        pieces = None
        for hop in range(parts - 1, -1, -1):
            part = (my_part + hop) % parts
            mine = lax.dynamic_index_in_dim(keep, part, 1, keepdims=False).astype(jnp.float32)
            mine += lax.dynamic_index_in_dim(got, part, 1, keepdims=False).astype(jnp.float32)
            if hop:
                across = [(i, (i + 2 * hop) % cmp_count) for i in range(cmp_count)]
                arrived = lax.ppermute(mine.astype(jnp.bfloat16), "cmp", across)
                arrived = arrived.astype(jnp.float32)
                pieces = arrived if pieces is None else pieces + arrived
            else:
                pieces = mine if pieces is None else pieces + mine
        done.append(jnp.transpose(pieces, (1, 0, 2)))
    shard = jnp.concatenate(done, axis=1)
    normal_blocks = shard[:, :, : near_count * mark_count].reshape(
        shard.shape[0], owned, near_count, mark_count
    )
    right_sides = shard[:, :, near_count * mark_count :]
    return (normal_blocks, right_sides)


def solution(mesh):
    placed = (
        P(("cmp", "lmk"), None),
        P(("cmp", "lmk"), None),
        P(("cmp", "lmk"), None),
        P("lmk", None, None),
        P(),
    )
    return jax.shard_map(
        on_device,
        mesh=mesh,
        in_specs=placed,
        out_specs=(P("cmp", "lmk", None, None), P("cmp", "lmk", None)),
        check_vma=False,
    )
```

```python
import functools
import math

import jax
import jax.numpy as jnp
from jax import lax
from jax.experimental import pallas as pl
from jax.experimental.pallas import tpu as pltpu
from jax.sharding import PartitionSpec as P

LIFT = 8.0
FLAG_LANES = 128
CHUNKS = 4


def normalize(data):
    wide = data.astype(jnp.float32)
    return (wide * lax.rsqrt(jnp.sum(wide * wide, axis=-1, keepdims=True) + 1e-06)).astype(
        jnp.bfloat16
    )


def dispatch_kernel(
    cluster_count, first_ref, lists_ref, rows_ref, out_ref, rank_ref, hit_ref
):
    sources, picks, count = lists_ref.shape
    owned, _, cap, _ = out_ref.shape
    width = rows_ref.shape[2] - FLAG_LANES
    rim = owned // 2
    extended = owned + 2 * rim
    step = pl.program_id(0)

    @pl.when(step == 0)
    def _():
        first = first_ref[0]
        index = lax.broadcasted_iota(jnp.int32, (FLAG_LANES, count), 0)
        ident = index + (first - rim + cluster_count)
        ident = jnp.where(ident >= cluster_count, ident - cluster_count, ident)
        ident = jnp.where(ident >= cluster_count, ident - cluster_count, ident)
        ident = jnp.where(index < extended, ident, -1)
        for source in range(sources):
            hit = lists_ref[source, 0:1, :] == ident
            for pick in range(1, picks):
                hit = hit | (lists_ref[source, pick : pick + 1, :] == ident)
            hit_ref[source] = jnp.where(hit, 1.0, 0.0).astype(jnp.bfloat16)
        before = lax.broadcasted_iota(jnp.int32, (count, count), 0) < lax.broadcasted_iota(
            jnp.int32, (count, count), 1
        )
        before = jnp.where(before, 1.0, 0.0).astype(jnp.bfloat16)
        own = hit_ref[:, rim : rim + owned, :].reshape(sources * owned, count)
        rank = jnp.dot(own, before, preferred_element_type=jnp.float32)
        rank = jnp.where(own.astype(jnp.float32) > 0.5, rank, -1.0)
        rank_ref[...] = rank.astype(jnp.int32).reshape(sources, owned, count)

    group = max(1, 256 // cap)
    slot = lax.broadcasted_iota(jnp.int32, (cap, count), 0)
    for start in range(0, owned, group):
        picked = jnp.concatenate(
            [
                jnp.where(rank_ref[step, pl.ds(start + k, 1), :] == slot, 1.0, 0.0).astype(
                    jnp.bfloat16
                )
                for k in range(group)
            ],
            axis=0,
        )
        moved = jnp.dot(picked, rows_ref[0], preferred_element_type=jnp.float32)
        flags = lax.dot_general(
            picked, hit_ref[step], (((1,), (1,)), ((), ())), preferred_element_type=jnp.float32
        )
        moved = moved.astype(jnp.bfloat16).reshape(group, cap, moved.shape[1])
        flags = flags.astype(jnp.bfloat16).reshape(group, cap, FLAG_LANES)
        out_ref[start : start + group, 0, :, :width] = moved[:, :, :width]
        out_ref[start : start + group, 0, :, width : width + FLAG_LANES] = flags
        out_ref[start : start + group, 0, :, width + FLAG_LANES :] = moved[:, :, width:]


def dispatch(first, lists, rows, owned, cap, cluster_count):
    sources, picks, count = lists.shape
    total = rows.shape[2] + FLAG_LANES
    return pl.pallas_call(
        functools.partial(dispatch_kernel, cluster_count),
        grid=(sources,),
        in_specs=[
            pl.BlockSpec(memory_space=pltpu.SMEM),
            pl.BlockSpec((sources, picks, count), lambda s: (0, 0, 0)),
            pl.BlockSpec((1, count, rows.shape[2]), lambda s: (s, 0, 0)),
        ],
        out_specs=pl.BlockSpec((owned, 1, cap, total), lambda s: (0, s, 0, 0)),
        out_shape=jax.ShapeDtypeStruct((owned, sources, cap, total), jnp.bfloat16),
        scratch_shapes=[
            pltpu.VMEM((sources, owned, count), jnp.int32),
            pltpu.VMEM((sources, FLAG_LANES, count), jnp.bfloat16),
        ],
        compiler_params=pltpu.CompilerParams(vmem_limit_bytes=48 * 2**20),
        cost_estimate=pl.CostEstimate(
            flops=2 * sources * owned * cap * count * total,
            bytes_accessed=2 * sources * (count * rows.shape[2] + owned * cap * total),
            transcendentals=0,
        ),
    )(first, lists, rows)


def block_kernel(base, near_count, scale, spots_ref, slots_ref, marks_ref, keep_ref, send_ref):
    mark_count = marks_ref.shape[1]
    depth = marks_ref.shape[2]
    parts, rows = keep_ref.shape[1], keep_ref.shape[2]
    cluster = base + pl.program_id(0)
    odd = spots_ref[spots_ref.shape[0] - 1] == 1
    factor = scale * math.log2(math.e)
    shift = LIFT * factor + 4.0 * math.log2(math.e)
    left = slots_ref[0, :, :depth]

    def kern(near_slot):
        marks = marks_ref[spots_ref[cluster * near_count + near_slot]]
        scores = lax.dot_general(
            left, marks, (((1,), (1,)), ((), ())), preferred_element_type=jnp.float32
        )
        return jnp.exp2(scores * factor - shift).astype(jnp.bfloat16)

    def store(block, column):
        width = block.shape[1]
        for part in range(parts):
            low = block[2 * part * rows : (2 * part + 1) * rows]
            high = block[(2 * part + 1) * rows : (2 * part + 2) * rows]
            keep_ref[0, part, :, column : column + width] = jnp.where(odd, high, low).astype(
                jnp.bfloat16
            )
            send_ref[0, part, :, column : column + width] = jnp.where(odd, low, high).astype(
                jnp.bfloat16
            )

    own = kern(0)
    turned = own.T
    for near_slot in range(near_count):
        other = own if near_slot == 0 else kern(near_slot)
        store(
            jnp.dot(turned, other, preferred_element_type=jnp.float32), near_slot * mark_count
        )
    store(
        jnp.dot(turned, slots_ref[0, :, depth:], preferred_element_type=jnp.float32),
        near_count * mark_count,
    )


def blocks(base, clusters, near_count, scale, parts, spots, slots, marks):
    mark_count, depth = marks.shape[1], marks.shape[2]
    slot_count = slots.shape[1]
    width = near_count * mark_count + slots.shape[2] - depth
    rows = mark_count // (2 * parts)
    shape = jax.ShapeDtypeStruct((clusters, parts, rows, width), jnp.bfloat16)
    spec = pl.BlockSpec((1, parts, rows, width), lambda a: (a, 0, 0, 0))
    return pl.pallas_call(
        functools.partial(block_kernel, base, near_count, scale),
        grid=(clusters,),
        in_specs=[
            pl.BlockSpec(memory_space=pltpu.SMEM),
            pl.BlockSpec((1, slot_count, slots.shape[2]), lambda a: (a + base, 0, 0)),
            pl.BlockSpec(marks.shape, lambda a: (0, 0, 0), pipeline_mode=pl.Buffered(1)),
        ],
        out_specs=[spec, spec],
        out_shape=[shape, shape],
        compiler_params=pltpu.CompilerParams(vmem_limit_bytes=48 * 2**20),
        cost_estimate=pl.CostEstimate(
            flops=2 * clusters * slot_count * width * (depth + mark_count),
            bytes_accessed=2 * marks.size + 2 * clusters * (slot_count * 768 + 256 * width),
            transcendentals=clusters * slot_count * width,
        ),
    )(spots, slots, marks)


def on_device(compounds, targets, cluster_lists, landmarks, neighbours):
    lmk_count = lax.axis_size("lmk")
    cmp_count = lax.axis_size("cmp")
    my_lmk = lax.axis_index("lmk")
    my_cmp = lax.axis_index("cmp")
    owned, mark_count, width = landmarks.shape
    rim = owned // 2
    near_count = neighbours.shape[1]
    cluster_count = neighbours.shape[0]
    cap = cluster_lists.shape[1] * (2 * compounds.shape[0] // cluster_count)
    scale = 0.75 * math.sqrt(width)
    first = my_lmk * owned

    rows = jnp.concatenate([normalize(compounds), targets], axis=1)
    count, lanes = rows.shape
    picks = cluster_lists.shape[1]
    per_pick = -(-count // lanes)
    listed = jnp.pad(cluster_lists.T.astype(jnp.bfloat16), ((0, 0), (0, per_pick * lanes - count)))
    listed = listed.reshape(picks * per_pick, lanes)
    listed = jnp.pad(listed, ((0, -(picks * per_pick) % 16), (0, 0)))
    all_rows = lax.all_gather(jnp.concatenate([rows, listed], axis=0), "lmk")
    all_lists = all_rows[:, count : count + picks * per_pick].reshape(lmk_count, picks, -1)
    all_lists = all_lists[:, :, :count].astype(jnp.int32)

    forward = [(i, (i + 1) % lmk_count) for i in range(lmk_count)]
    backward = [(target, source) for source, target in forward]
    unit_marks = normalize(landmarks)
    low = lax.ppermute(unit_marks[owned - rim :], "lmk", forward)
    high = lax.ppermute(unit_marks[:rim], "lmk", backward)
    extended = jnp.concatenate([low, unit_marks, high], axis=0)
    lift = jnp.where(
        jnp.arange(owned + 2 * rim)[:, None, None] == jnp.arange(FLAG_LANES)[None, None, :],
        LIFT,
        0.0,
    ).astype(jnp.bfloat16)
    lift = jnp.broadcast_to(lift, (owned + 2 * rim, mark_count, FLAG_LANES))
    extended = jnp.concatenate([extended, lift], axis=2)

    near = lax.dynamic_slice_in_dim(neighbours, first, owned, 0)
    spots = jnp.mod(near - first + rim, cluster_count).reshape(-1)
    my_core = my_cmp % 2
    my_part = my_cmp // 2
    spots = jnp.concatenate([spots, my_core[None]]).astype(jnp.int32)

    slots = dispatch(
        jnp.asarray(first, jnp.int32)[None], all_lists, all_rows, owned, cap, cluster_count
    )
    slots = slots.reshape(owned, lmk_count * cap, slots.shape[3])
    parts = cmp_count // 2
    cores = [(i, i ^ 1) for i in range(cmp_count)]
    each = owned // CHUNKS
    done = []
    held = []
    for chunk in range(CHUNKS):
        if chunk > 1:
            spots, *held[chunk - 2] = lax.optimization_barrier((spots, *held[chunk - 2]))
        keep, send = blocks(
            chunk * each, each, near_count, scale, parts, spots, slots, extended
        )
        got = lax.ppermute(send, "cmp", cores)
        sums = []
        for hop in range(parts):
            part = (my_part + hop) % parts
            mine = lax.dynamic_index_in_dim(keep, part, 1, keepdims=False).astype(jnp.float32)
            mine += lax.dynamic_index_in_dim(got, part, 1, keepdims=False).astype(jnp.float32)
            sums.append(mine.astype(jnp.bfloat16) if hop else mine)
        held.append(sums)
    for sums in held:
        pieces = sums[0]
        for hop in range(1, parts):
            across = [(i, (i + 2 * hop) % cmp_count) for i in range(cmp_count)]
            pieces += lax.ppermute(sums[hop], "cmp", across).astype(jnp.float32)
        done.append(jnp.transpose(pieces, (1, 0, 2)))
    shard = jnp.concatenate(done, axis=1)
    normal_blocks = shard[:, :, : near_count * mark_count].reshape(
        shard.shape[0], owned, near_count, mark_count
    )
    right_sides = shard[:, :, near_count * mark_count :]
    return (normal_blocks, right_sides)


def solution(mesh):
    placed = (
        P(("cmp", "lmk"), None),
        P(("cmp", "lmk"), None),
        P(("cmp", "lmk"), None),
        P("lmk", None, None),
        P(),
    )
    return jax.shard_map(
        on_device,
        mesh=mesh,
        in_specs=placed,
        out_specs=(P("cmp", "lmk", None, None), P("cmp", "lmk", None)),
        check_vma=False,
    )
```

```python
import functools
import math

import jax
import jax.numpy as jnp
from jax import lax
from jax.experimental import pallas as pl
from jax.experimental.pallas import tpu as pltpu
from jax.sharding import PartitionSpec as P

LIFT = 8.0
FLAG_LANES = 128
CHUNKS = 8


def normalize(data):
    wide = data.astype(jnp.float32)
    return (wide * lax.rsqrt(jnp.sum(wide * wide, axis=-1, keepdims=True) + 1e-06)).astype(
        jnp.bfloat16
    )


def dispatch_kernel(
    cluster_count, first_ref, lists_ref, rows_ref, out_ref, rank_ref, hit_ref
):
    sources, picks, count = lists_ref.shape
    owned, _, cap, _ = out_ref.shape
    width = rows_ref.shape[2] - FLAG_LANES
    rim = owned // 2
    extended = owned + 2 * rim
    step = pl.program_id(0)

    @pl.when(step == 0)
    def _():
        first = first_ref[0]
        index = lax.broadcasted_iota(jnp.int32, (FLAG_LANES, count), 0)
        ident = index + (first - rim + cluster_count)
        ident = jnp.where(ident >= cluster_count, ident - cluster_count, ident)
        ident = jnp.where(ident >= cluster_count, ident - cluster_count, ident)
        ident = jnp.where(index < extended, ident, -1)
        for source in range(sources):
            hit = lists_ref[source, 0:1, :] == ident
            for pick in range(1, picks):
                hit = hit | (lists_ref[source, pick : pick + 1, :] == ident)
            hit_ref[source] = jnp.where(hit, 1.0, 0.0).astype(jnp.bfloat16)
        before = lax.broadcasted_iota(jnp.int32, (count, count), 0) < lax.broadcasted_iota(
            jnp.int32, (count, count), 1
        )
        before = jnp.where(before, 1.0, 0.0).astype(jnp.bfloat16)
        own = hit_ref[:, rim : rim + owned, :].reshape(sources * owned, count)
        rank = jnp.dot(own, before, preferred_element_type=jnp.float32)
        rank = jnp.where(own.astype(jnp.float32) > 0.5, rank, -1.0)
        rank_ref[...] = rank.astype(jnp.int32).reshape(sources, owned, count)

    group = max(1, 256 // cap)
    slot = lax.broadcasted_iota(jnp.int32, (cap, count), 0)
    for start in range(0, owned, group):
        picked = jnp.concatenate(
            [
                jnp.where(rank_ref[step, pl.ds(start + k, 1), :] == slot, 1.0, 0.0).astype(
                    jnp.bfloat16
                )
                for k in range(group)
            ],
            axis=0,
        )
        moved = jnp.dot(picked, rows_ref[0], preferred_element_type=jnp.float32)
        flags = lax.dot_general(
            picked, hit_ref[step], (((1,), (1,)), ((), ())), preferred_element_type=jnp.float32
        )
        moved = moved.astype(jnp.bfloat16).reshape(group, cap, moved.shape[1])
        flags = flags.astype(jnp.bfloat16).reshape(group, cap, FLAG_LANES)
        out_ref[start : start + group, 0, :, :width] = moved[:, :, :width]
        out_ref[start : start + group, 0, :, width : width + FLAG_LANES] = flags
        out_ref[start : start + group, 0, :, width + FLAG_LANES :] = moved[:, :, width:]


def dispatch(first, lists, rows, owned, cap, cluster_count):
    sources, picks, count = lists.shape
    total = rows.shape[2] + FLAG_LANES
    return pl.pallas_call(
        functools.partial(dispatch_kernel, cluster_count),
        grid=(sources,),
        in_specs=[
            pl.BlockSpec(memory_space=pltpu.SMEM),
            pl.BlockSpec((sources, picks, count), lambda s: (0, 0, 0)),
            pl.BlockSpec((1, count, rows.shape[2]), lambda s: (s, 0, 0)),
        ],
        out_specs=pl.BlockSpec((owned, 1, cap, total), lambda s: (0, s, 0, 0)),
        out_shape=jax.ShapeDtypeStruct((owned, sources, cap, total), jnp.bfloat16),
        scratch_shapes=[
            pltpu.VMEM((sources, owned, count), jnp.int32),
            pltpu.VMEM((sources, FLAG_LANES, count), jnp.bfloat16),
        ],
        compiler_params=pltpu.CompilerParams(vmem_limit_bytes=48 * 2**20),
        cost_estimate=pl.CostEstimate(
            flops=2 * sources * owned * cap * count * total,
            bytes_accessed=2 * sources * (count * rows.shape[2] + owned * cap * total),
            transcendentals=0,
        ),
    )(first, lists, rows)


def block_kernel(base, near_count, scale, spots_ref, slots_ref, marks_ref, keep_ref, send_ref):
    mark_count = marks_ref.shape[1]
    depth = marks_ref.shape[2]
    parts, rows = keep_ref.shape[1], keep_ref.shape[2]
    cluster = base + pl.program_id(0)
    odd = spots_ref[spots_ref.shape[0] - 1] == 1
    factor = scale * math.log2(math.e)
    shift = LIFT * factor + 4.0 * math.log2(math.e)
    left = slots_ref[0, :, :depth]

    def kern(near_slot):
        marks = marks_ref[spots_ref[cluster * near_count + near_slot]]
        scores = lax.dot_general(
            left, marks, (((1,), (1,)), ((), ())), preferred_element_type=jnp.float32
        )
        return jnp.exp2(scores * factor - shift).astype(jnp.bfloat16)

    def store(block, column):
        width = block.shape[1]
        for part in range(parts):
            low = block[2 * part * rows : (2 * part + 1) * rows]
            high = block[(2 * part + 1) * rows : (2 * part + 2) * rows]
            keep_ref[0, part, :, column : column + width] = jnp.where(odd, high, low).astype(
                jnp.bfloat16
            )
            send_ref[0, part, :, column : column + width] = jnp.where(odd, low, high).astype(
                jnp.bfloat16
            )

    own = kern(0)
    turned = own.T
    for near_slot in range(near_count):
        other = own if near_slot == 0 else kern(near_slot)
        store(
            jnp.dot(turned, other, preferred_element_type=jnp.float32), near_slot * mark_count
        )
    store(
        jnp.dot(turned, slots_ref[0, :, depth:], preferred_element_type=jnp.float32),
        near_count * mark_count,
    )


def blocks(base, clusters, near_count, scale, parts, spots, slots, marks):
    mark_count, depth = marks.shape[1], marks.shape[2]
    slot_count = slots.shape[1]
    width = near_count * mark_count + slots.shape[2] - depth
    rows = mark_count // (2 * parts)
    shape = jax.ShapeDtypeStruct((clusters, parts, rows, width), jnp.bfloat16)
    spec = pl.BlockSpec((1, parts, rows, width), lambda a: (a, 0, 0, 0))
    return pl.pallas_call(
        functools.partial(block_kernel, base, near_count, scale),
        grid=(clusters,),
        in_specs=[
            pl.BlockSpec(memory_space=pltpu.SMEM),
            pl.BlockSpec((1, slot_count, slots.shape[2]), lambda a: (a + base, 0, 0)),
            pl.BlockSpec(marks.shape, lambda a: (0, 0, 0), pipeline_mode=pl.Buffered(1)),
        ],
        out_specs=[spec, spec],
        out_shape=[shape, shape],
        compiler_params=pltpu.CompilerParams(vmem_limit_bytes=48 * 2**20),
        cost_estimate=pl.CostEstimate(
            flops=2**20,
            bytes_accessed=2**20,
            transcendentals=0,
        ),
    )(spots, slots, marks)


def on_device(compounds, targets, cluster_lists, landmarks, neighbours):
    lmk_count = lax.axis_size("lmk")
    cmp_count = lax.axis_size("cmp")
    my_lmk = lax.axis_index("lmk")
    my_cmp = lax.axis_index("cmp")
    owned, mark_count, width = landmarks.shape
    rim = owned // 2
    near_count = neighbours.shape[1]
    cluster_count = neighbours.shape[0]
    cap = cluster_lists.shape[1] * (2 * compounds.shape[0] // cluster_count)
    scale = 0.75 * math.sqrt(width)
    first = my_lmk * owned

    rows = jnp.concatenate([normalize(compounds), targets], axis=1)
    count, lanes = rows.shape
    picks = cluster_lists.shape[1]
    per_pick = -(-count // lanes)
    listed = jnp.pad(cluster_lists.T.astype(jnp.bfloat16), ((0, 0), (0, per_pick * lanes - count)))
    listed = listed.reshape(picks * per_pick, lanes)
    listed = jnp.pad(listed, ((0, -(picks * per_pick) % 16), (0, 0)))
    all_rows = lax.all_gather(jnp.concatenate([rows, listed], axis=0), "lmk")
    all_lists = all_rows[:, count : count + picks * per_pick].reshape(lmk_count, picks, -1)
    all_lists = all_lists[:, :, :count].astype(jnp.int32)

    forward = [(i, (i + 1) % lmk_count) for i in range(lmk_count)]
    backward = [(target, source) for source, target in forward]
    unit_marks = normalize(landmarks)
    portion = mark_count // cmp_count
    quarter = lax.dynamic_slice_in_dim(unit_marks, my_cmp * portion, portion, 1)
    low = lax.ppermute(quarter[owned - rim :], "lmk", forward)
    high = lax.ppermute(quarter[:rim], "lmk", backward)
    rims = jnp.concatenate([low, high], axis=0)
    edges = jnp.zeros((2 * rim, cmp_count, portion, width), jnp.bfloat16)
    for turn in range(cmp_count):
        swap = [(i, i ^ turn) for i in range(cmp_count)]
        piece = lax.ppermute(rims, "cmp", swap) if turn else rims
        edges = lax.dynamic_update_slice_in_dim(
            edges, piece[:, None], jnp.bitwise_xor(my_cmp, turn), 1
        )
    edges = edges.reshape(2 * rim, mark_count, width)
    extended = jnp.concatenate([edges[:rim], unit_marks, edges[rim:]], axis=0)
    lift = jnp.where(
        jnp.arange(owned + 2 * rim)[:, None, None] == jnp.arange(FLAG_LANES)[None, None, :],
        LIFT,
        0.0,
    ).astype(jnp.bfloat16)
    lift = jnp.broadcast_to(lift, (owned + 2 * rim, mark_count, FLAG_LANES))
    extended = jnp.concatenate([extended, lift], axis=2)

    near = lax.dynamic_slice_in_dim(neighbours, first, owned, 0)
    spots = jnp.mod(near - first + rim, cluster_count).reshape(-1)
    my_core = my_cmp % 2
    my_part = my_cmp // 2
    spots = jnp.concatenate([spots, my_core[None]]).astype(jnp.int32)

    slots = dispatch(
        jnp.asarray(first, jnp.int32)[None], all_lists, all_rows, owned, cap, cluster_count
    )
    slots = slots.reshape(owned, lmk_count * cap, slots.shape[3])
    parts = cmp_count // 2
    cores = [(i, i ^ 1) for i in range(cmp_count)]
    each = owned // CHUNKS
    done = []
    held = []
    crossed = []

    def cross(sums):
        pieces = []
        for hop in range(1, parts):
            across = [(i, (i + 2 * hop) % cmp_count) for i in range(cmp_count)]
            pieces.append(lax.ppermute(sums[hop], "cmp", across))
        return pieces

    for chunk in range(CHUNKS):
        if chunk > 1:
            spots, *held[chunk - 2] = lax.optimization_barrier((spots, *held[chunk - 2]))
            crossed.append(cross(held[chunk - 2]))
        if chunk > 2:
            spots, *crossed[chunk - 3] = lax.optimization_barrier((spots, *crossed[chunk - 3]))
        keep, send = blocks(
            chunk * each, each, near_count, scale, parts, spots, slots, extended
        )
        got = lax.ppermute(send, "cmp", cores)
        sums = []
        for hop in range(parts):
            part = (my_part + hop) % parts
            mine = lax.dynamic_index_in_dim(keep, part, 1, keepdims=False).astype(jnp.float32)
            mine += lax.dynamic_index_in_dim(got, part, 1, keepdims=False).astype(jnp.float32)
            sums.append(mine.astype(jnp.bfloat16) if hop else mine)
        held.append(sums)
    crossed += [cross(sums) for sums in held[len(crossed) :]]
    for sums, arrived in zip(held, crossed):
        pieces = sums[0]
        for piece in arrived:
            pieces += piece.astype(jnp.float32)
        done.append(jnp.transpose(pieces, (1, 0, 2)))
    shard = jnp.concatenate(done, axis=1)
    normal_blocks = shard[:, :, : near_count * mark_count].reshape(
        shard.shape[0], owned, near_count, mark_count
    )
    right_sides = shard[:, :, near_count * mark_count :]
    return (normal_blocks, right_sides)


def solution(mesh):
    placed = (
        P(("cmp", "lmk"), None),
        P(("cmp", "lmk"), None),
        P(("cmp", "lmk"), None),
        P("lmk", None, None),
        P(),
    )
    return jax.shard_map(
        on_device,
        mesh=mesh,
        in_specs=placed,
        out_specs=(P("cmp", "lmk", None, None), P("cmp", "lmk", None)),
        check_vma=False,
    )
```

```python
import functools
import math

import jax
import jax.numpy as jnp
from jax import lax
from jax.experimental import pallas as pl
from jax.experimental.pallas import tpu as pltpu
from jax.sharding import PartitionSpec as P

LIFT = 8.0
FLAG_LANES = 128
CHUNKS = 8


def normalize(data):
    wide = data.astype(jnp.float32)
    return (wide * lax.rsqrt(jnp.sum(wide * wide, axis=-1, keepdims=True) + 1e-06)).astype(
        jnp.bfloat16
    )


def dispatch_kernel(
    cluster_count, first_ref, lists_ref, rows_ref, out_ref, rank_ref, hit_ref
):
    sources, picks, count = lists_ref.shape
    owned, _, cap, _ = out_ref.shape
    width = rows_ref.shape[2] - FLAG_LANES
    rim = owned // 2
    extended = owned + 2 * rim
    step = pl.program_id(0)

    @pl.when(step == 0)
    def _():
        first = first_ref[0]
        index = lax.broadcasted_iota(jnp.int32, (FLAG_LANES, count), 0)
        ident = index + (first - rim + cluster_count)
        ident = jnp.where(ident >= cluster_count, ident - cluster_count, ident)
        ident = jnp.where(ident >= cluster_count, ident - cluster_count, ident)
        ident = jnp.where(index < extended, ident, -1)
        for source in range(sources):
            hit = lists_ref[source, 0:1, :] == ident
            for pick in range(1, picks):
                hit = hit | (lists_ref[source, pick : pick + 1, :] == ident)
            hit_ref[source] = jnp.where(hit, 1.0, 0.0).astype(jnp.bfloat16)
        before = lax.broadcasted_iota(jnp.int32, (count, count), 0) < lax.broadcasted_iota(
            jnp.int32, (count, count), 1
        )
        before = jnp.where(before, 1.0, 0.0).astype(jnp.bfloat16)
        own = hit_ref[:, rim : rim + owned, :].reshape(sources * owned, count)
        rank = jnp.dot(own, before, preferred_element_type=jnp.float32)
        rank = jnp.where(own.astype(jnp.float32) > 0.5, rank, -1.0)
        rank_ref[...] = rank.astype(jnp.int32).reshape(sources, owned, count)

    group = max(1, 256 // cap)
    slot = lax.broadcasted_iota(jnp.int32, (cap, count), 0)
    for start in range(0, owned, group):
        picked = jnp.concatenate(
            [
                jnp.where(rank_ref[step, pl.ds(start + k, 1), :] == slot, 1.0, 0.0).astype(
                    jnp.bfloat16
                )
                for k in range(group)
            ],
            axis=0,
        )
        moved = jnp.dot(picked, rows_ref[0], preferred_element_type=jnp.float32)
        flags = lax.dot_general(
            picked, hit_ref[step], (((1,), (1,)), ((), ())), preferred_element_type=jnp.float32
        )
        moved = moved.astype(jnp.bfloat16).reshape(group, cap, moved.shape[1])
        flags = flags.astype(jnp.bfloat16).reshape(group, cap, FLAG_LANES)
        out_ref[start : start + group, 0, :, :width] = moved[:, :, :width]
        out_ref[start : start + group, 0, :, width : width + FLAG_LANES] = flags
        out_ref[start : start + group, 0, :, width + FLAG_LANES :] = moved[:, :, width:]


def dispatch(first, lists, rows, owned, cap, cluster_count, number, held):
    sources, picks, count = lists.shape
    total = rows.shape[2] + FLAG_LANES
    kernel = functools.partial(dispatch_kernel, cluster_count)
    in_specs = [
        pl.BlockSpec(memory_space=pltpu.SMEM),
        pl.BlockSpec((sources, picks, count), lambda s: (0, 0, 0)),
        pl.BlockSpec((1, count, rows.shape[2]), lambda s: (s, 0, 0)),
    ]
    operands = [first, lists, rows]
    aliases = {}
    body = kernel
    if held is not None:
        in_specs.append(pl.BlockSpec(memory_space=pl.ANY))
        operands.append(held)
        aliases = {3: 0}

        def body(first_ref, lists_ref, rows_ref, held_ref, out_ref, rank_ref, hit_ref):
            kernel(first_ref, lists_ref, rows_ref, out_ref, rank_ref, hit_ref)

    return pl.pallas_call(
        body,
        grid=(sources,),
        in_specs=in_specs,
        out_specs=pl.BlockSpec(
            (owned, 1, cap, total), lambda s: (0, s + number * sources, 0, 0)
        ),
        out_shape=jax.ShapeDtypeStruct((owned, 2 * sources, cap, total), jnp.bfloat16),
        scratch_shapes=[
            pltpu.VMEM((sources, owned, count), jnp.int32),
            pltpu.VMEM((sources, FLAG_LANES, count), jnp.bfloat16),
        ],
        input_output_aliases=aliases,
        compiler_params=pltpu.CompilerParams(vmem_limit_bytes=48 * 2**20),
        cost_estimate=pl.CostEstimate(
            flops=2 * sources * owned * cap * count * total,
            bytes_accessed=2 * sources * (count * rows.shape[2] + owned * cap * total),
            transcendentals=0,
        ),
    )(*operands)


def block_kernel(base, near_count, scale, spots_ref, slots_ref, marks_ref, keep_ref, send_ref):
    mark_count = marks_ref.shape[1]
    depth = marks_ref.shape[2]
    parts, rows = keep_ref.shape[1], keep_ref.shape[2]
    cluster = base + pl.program_id(0)
    odd = spots_ref[spots_ref.shape[0] - 1] == 1
    factor = scale * math.log2(math.e)
    shift = LIFT * factor + 4.0 * math.log2(math.e)
    left = slots_ref[0, :, :depth]

    def kern(near_slot):
        marks = marks_ref[spots_ref[cluster * near_count + near_slot]]
        scores = lax.dot_general(
            left, marks, (((1,), (1,)), ((), ())), preferred_element_type=jnp.float32
        )
        return jnp.exp2(scores * factor - shift).astype(jnp.bfloat16)

    def store(block, column):
        width = block.shape[1]
        for part in range(parts):
            low = block[2 * part * rows : (2 * part + 1) * rows]
            high = block[(2 * part + 1) * rows : (2 * part + 2) * rows]
            keep_ref[0, part, :, column : column + width] = jnp.where(odd, high, low).astype(
                jnp.bfloat16
            )
            send_ref[0, part, :, column : column + width] = jnp.where(odd, low, high).astype(
                jnp.bfloat16
            )

    own = kern(0)
    turned = own.T
    for near_slot in range(near_count):
        other = own if near_slot == 0 else kern(near_slot)
        store(
            jnp.dot(turned, other, preferred_element_type=jnp.float32), near_slot * mark_count
        )
    store(
        jnp.dot(turned, slots_ref[0, :, depth:], preferred_element_type=jnp.float32),
        near_count * mark_count,
    )


def blocks(base, clusters, near_count, scale, parts, spots, slots, marks):
    mark_count, depth = marks.shape[1], marks.shape[2]
    slot_count = slots.shape[1]
    width = near_count * mark_count + slots.shape[2] - depth
    rows = mark_count // (2 * parts)
    shape = jax.ShapeDtypeStruct((clusters, parts, rows, width), jnp.bfloat16)
    spec = pl.BlockSpec((1, parts, rows, width), lambda a: (a, 0, 0, 0))
    return pl.pallas_call(
        functools.partial(block_kernel, base, near_count, scale),
        grid=(clusters,),
        in_specs=[
            pl.BlockSpec(memory_space=pltpu.SMEM),
            pl.BlockSpec((1, slot_count, slots.shape[2]), lambda a: (a + base, 0, 0)),
            pl.BlockSpec(marks.shape, lambda a: (0, 0, 0), pipeline_mode=pl.Buffered(1)),
        ],
        out_specs=[spec, spec],
        out_shape=[shape, shape],
        compiler_params=pltpu.CompilerParams(vmem_limit_bytes=48 * 2**20),
        cost_estimate=pl.CostEstimate(
            flops=2**20,
            bytes_accessed=2**20,
            transcendentals=0,
        ),
    )(spots, slots, marks)


def on_device(compounds, targets, cluster_lists, landmarks, neighbours):
    lmk_count = lax.axis_size("lmk")
    cmp_count = lax.axis_size("cmp")
    my_lmk = lax.axis_index("lmk")
    my_cmp = lax.axis_index("cmp")
    owned, mark_count, width = landmarks.shape
    rim = owned // 2
    near_count = neighbours.shape[1]
    cluster_count = neighbours.shape[0]
    cap = cluster_lists.shape[1] * (2 * compounds.shape[0] // cluster_count)
    scale = 0.75 * math.sqrt(width)
    first = my_lmk * owned

    rows = jnp.concatenate([normalize(compounds), targets], axis=1)
    count, lanes = rows.shape
    picks = cluster_lists.shape[1]
    per_pick = -(-count // lanes)
    listed = jnp.pad(cluster_lists.T.astype(jnp.bfloat16), ((0, 0), (0, per_pick * lanes - count)))
    listed = listed.reshape(picks * per_pick, lanes)
    listed = jnp.pad(listed, ((0, -(picks * per_pick) % 16), (0, 0)))
    own = jnp.concatenate([rows, listed], axis=0)
    inner = lmk_count // 4

    def shifted(data, outer):
        return lax.ppermute(data, "lmk", [(i, i ^ (outer * inner)) for i in range(lmk_count)])

    def spread(data):
        gathered = [data]
        for turn in range(1, inner):
            pairs = [(i, i - i % inner + (i % inner + turn) % inner) for i in range(lmk_count)]
            gathered.append(lax.ppermute(data, "lmk", pairs))
        return gathered

    near_z = shifted(own, 1)
    far_z = shifted(own, 2)
    halves = [
        jnp.stack(spread(own) + spread(near_z)),
        jnp.stack(spread(far_z) + spread(shifted(near_z, 2))),
    ]

    def lists_of(half):
        taken = half[:, count : count + picks * per_pick].reshape(half.shape[0], picks, -1)
        return taken[:, :, :count].astype(jnp.int32)

    forward = [(i, (i + 1) % lmk_count) for i in range(lmk_count)]
    backward = [(target, source) for source, target in forward]
    unit_marks = normalize(landmarks)
    portion = mark_count // cmp_count
    quarter = lax.dynamic_slice_in_dim(unit_marks, my_cmp * portion, portion, 1)
    low = lax.ppermute(quarter[owned - rim :], "lmk", forward)
    high = lax.ppermute(quarter[:rim], "lmk", backward)
    rims = jnp.concatenate([low, high], axis=0)
    edges = jnp.zeros((2 * rim, cmp_count, portion, width), jnp.bfloat16)
    for turn in range(cmp_count):
        swap = [(i, i ^ turn) for i in range(cmp_count)]
        piece = lax.ppermute(rims, "cmp", swap) if turn else rims
        edges = lax.dynamic_update_slice_in_dim(
            edges, piece[:, None], jnp.bitwise_xor(my_cmp, turn), 1
        )
    edges = edges.reshape(2 * rim, mark_count, width)
    extended = jnp.concatenate([edges[:rim], unit_marks, edges[rim:]], axis=0)
    lift = jnp.where(
        jnp.arange(owned + 2 * rim)[:, None, None] == jnp.arange(FLAG_LANES)[None, None, :],
        LIFT,
        0.0,
    ).astype(jnp.bfloat16)
    lift = jnp.broadcast_to(lift, (owned + 2 * rim, mark_count, FLAG_LANES))
    extended = jnp.concatenate([extended, lift], axis=2)

    near = lax.dynamic_slice_in_dim(neighbours, first, owned, 0)
    spots = jnp.mod(near - first + rim, cluster_count).reshape(-1)
    my_core = my_cmp % 2
    my_part = my_cmp // 2
    spots = jnp.concatenate([spots, my_core[None]]).astype(jnp.int32)

    slots = None
    for number, half in enumerate(halves):
        slots = dispatch(
            jnp.asarray(first, jnp.int32)[None],
            lists_of(half),
            half,
            owned,
            cap,
            cluster_count,
            number,
            slots,
        )
    slots = slots.reshape(owned, lmk_count * cap, slots.shape[3])
    parts = cmp_count // 2
    cores = [(i, i ^ 1) for i in range(cmp_count)]
    each = owned // CHUNKS
    done = []
    held = []
    crossed = []

    def cross(sums):
        pieces = []
        for hop in range(1, parts):
            across = [(i, (i + 2 * hop) % cmp_count) for i in range(cmp_count)]
            pieces.append(lax.ppermute(sums[hop], "cmp", across))
        return pieces

    for chunk in range(CHUNKS):
        if chunk > 1:
            spots, *held[chunk - 2] = lax.optimization_barrier((spots, *held[chunk - 2]))
            crossed.append(cross(held[chunk - 2]))
        if chunk > 2:
            spots, *crossed[chunk - 3] = lax.optimization_barrier((spots, *crossed[chunk - 3]))
        keep, send = blocks(
            chunk * each, each, near_count, scale, parts, spots, slots, extended
        )
        got = lax.ppermute(send, "cmp", cores)
        sums = []
        for hop in range(parts):
            part = (my_part + hop) % parts
            mine = lax.dynamic_index_in_dim(keep, part, 1, keepdims=False).astype(jnp.float32)
            mine += lax.dynamic_index_in_dim(got, part, 1, keepdims=False).astype(jnp.float32)
            sums.append(mine.astype(jnp.bfloat16) if hop else mine)
        held.append(sums)
    crossed += [cross(sums) for sums in held[len(crossed) :]]
    for sums, arrived in zip(held, crossed):
        pieces = sums[0]
        for piece in arrived:
            pieces += piece.astype(jnp.float32)
        done.append(jnp.transpose(pieces, (1, 0, 2)))
    shard = jnp.concatenate(done, axis=1)
    normal_blocks = shard[:, :, : near_count * mark_count].reshape(
        shard.shape[0], owned, near_count, mark_count
    )
    right_sides = shard[:, :, near_count * mark_count :]
    return (normal_blocks, right_sides)


def solution(mesh):
    placed = (
        P(("cmp", "lmk"), None),
        P(("cmp", "lmk"), None),
        P(("cmp", "lmk"), None),
        P("lmk", None, None),
        P(),
    )
    return jax.shard_map(
        on_device,
        mesh=mesh,
        in_specs=placed,
        out_specs=(P("cmp", "lmk", None, None), P("cmp", "lmk", None)),
        check_vma=False,
    )
```

```python
import functools
import math

import jax
import jax.numpy as jnp
from jax import lax
from jax.experimental import pallas as pl
from jax.experimental.pallas import tpu as pltpu
from jax.sharding import PartitionSpec as P

LIFT = 8.0
FLAG_LANES = 128
CHUNKS = 8


def normalize(data):
    wide = data.astype(jnp.float32)
    return (wide * lax.rsqrt(jnp.sum(wide * wide, axis=-1, keepdims=True) + 1e-06)).astype(
        jnp.bfloat16
    )


def dispatch_kernel(
    cluster_count, first_ref, lists_ref, rows_ref, out_ref, rank_ref, hit_ref
):
    sources, picks, count = lists_ref.shape
    owned, _, cap, _ = out_ref.shape
    width = rows_ref.shape[2] - FLAG_LANES
    rim = owned // 2
    extended = owned + 2 * rim
    step = pl.program_id(0)

    @pl.when(step == 0)
    def _():
        first = first_ref[0]
        index = lax.broadcasted_iota(jnp.int32, (FLAG_LANES, count), 0)
        ident = index + (first - rim + cluster_count)
        ident = jnp.where(ident >= cluster_count, ident - cluster_count, ident)
        ident = jnp.where(ident >= cluster_count, ident - cluster_count, ident)
        ident = jnp.where(index < extended, ident, -1)
        for source in range(sources):
            hit = lists_ref[source, 0:1, :] == ident
            for pick in range(1, picks):
                hit = hit | (lists_ref[source, pick : pick + 1, :] == ident)
            hit_ref[source] = jnp.where(hit, 1.0, 0.0).astype(jnp.bfloat16)
        before = lax.broadcasted_iota(jnp.int32, (count, count), 0) < lax.broadcasted_iota(
            jnp.int32, (count, count), 1
        )
        before = jnp.where(before, 1.0, 0.0).astype(jnp.bfloat16)
        own = hit_ref[:, rim : rim + owned, :].reshape(sources * owned, count)
        rank = jnp.dot(own, before, preferred_element_type=jnp.float32)
        rank = jnp.where(own.astype(jnp.float32) > 0.5, rank, -1.0)
        rank_ref[...] = rank.astype(jnp.int32).reshape(sources, owned, count)

    group = max(1, 256 // cap)
    slot = lax.broadcasted_iota(jnp.int32, (cap, count), 0)
    for start in range(0, owned, group):
        picked = jnp.concatenate(
            [
                jnp.where(rank_ref[step, pl.ds(start + k, 1), :] == slot, 1.0, 0.0).astype(
                    jnp.bfloat16
                )
                for k in range(group)
            ],
            axis=0,
        )
        moved = jnp.dot(picked, rows_ref[0], preferred_element_type=jnp.float32)
        flags = lax.dot_general(
            picked, hit_ref[step], (((1,), (1,)), ((), ())), preferred_element_type=jnp.float32
        )
        moved = moved.astype(jnp.bfloat16).reshape(group, cap, moved.shape[1])
        flags = flags.astype(jnp.bfloat16).reshape(group, cap, FLAG_LANES)
        out_ref[start : start + group, 0, :, :width] = moved[:, :, :width]
        out_ref[start : start + group, 0, :, width : width + FLAG_LANES] = flags
        out_ref[start : start + group, 0, :, width + FLAG_LANES :] = moved[:, :, width:]


def dispatch(first, lists, rows, owned, cap, cluster_count):
    sources, picks, count = lists.shape
    total = rows.shape[2] + FLAG_LANES
    return pl.pallas_call(
        functools.partial(dispatch_kernel, cluster_count),
        grid=(sources,),
        in_specs=[
            pl.BlockSpec(memory_space=pltpu.SMEM),
            pl.BlockSpec((sources, picks, count), lambda s: (0, 0, 0)),
            pl.BlockSpec((1, count, rows.shape[2]), lambda s: (s, 0, 0)),
        ],
        out_specs=pl.BlockSpec((owned, 1, cap, total), lambda s: (0, s, 0, 0)),
        out_shape=jax.ShapeDtypeStruct((owned, sources, cap, total), jnp.bfloat16),
        scratch_shapes=[
            pltpu.VMEM((sources, owned, count), jnp.int32),
            pltpu.VMEM((sources, FLAG_LANES, count), jnp.bfloat16),
        ],
        compiler_params=pltpu.CompilerParams(vmem_limit_bytes=48 * 2**20),
        cost_estimate=pl.CostEstimate(
            flops=2 * sources * owned * cap * count * total,
            bytes_accessed=2 * sources * (count * rows.shape[2] + owned * cap * total),
            transcendentals=0,
        ),
    )(first, lists, rows)


def block_kernel(base, near_count, scale, spots_ref, slots_ref, marks_ref, keep_ref, send_ref):
    mark_count = marks_ref.shape[1]
    depth = marks_ref.shape[2]
    parts, rows = keep_ref.shape[1], keep_ref.shape[2]
    cluster = base + pl.program_id(0)
    odd = spots_ref[spots_ref.shape[0] - 1] == 1
    factor = scale * math.log2(math.e)
    shift = LIFT * factor + 4.0 * math.log2(math.e)
    left = slots_ref[0, :, :depth]

    def kern(near_slot):
        marks = marks_ref[spots_ref[cluster * near_count + near_slot] - base]
        scores = lax.dot_general(
            left, marks, (((1,), (1,)), ((), ())), preferred_element_type=jnp.float32
        )
        return jnp.exp2(scores * factor - shift).astype(jnp.bfloat16)

    def store(block, column):
        width = block.shape[1]
        for part in range(parts):
            low = block[2 * part * rows : (2 * part + 1) * rows]
            high = block[(2 * part + 1) * rows : (2 * part + 2) * rows]
            keep_ref[0, part, :, column : column + width] = jnp.where(odd, high, low).astype(
                jnp.bfloat16
            )
            send_ref[0, part, :, column : column + width] = jnp.where(odd, low, high).astype(
                jnp.bfloat16
            )

    own = kern(0)
    turned = own.T
    for near_slot in range(near_count):
        other = own if near_slot == 0 else kern(near_slot)
        store(
            jnp.dot(turned, other, preferred_element_type=jnp.float32), near_slot * mark_count
        )
    store(
        jnp.dot(turned, slots_ref[0, :, depth:], preferred_element_type=jnp.float32),
        near_count * mark_count,
    )


def blocks(base, clusters, near_count, scale, parts, spots, slots, marks):
    mark_count, depth = marks.shape[1], marks.shape[2]
    slot_count = slots.shape[1]
    width = near_count * mark_count + slots.shape[2] - depth
    rows = mark_count // (2 * parts)
    window = marks.shape[0] - slots.shape[0] + clusters
    shape = jax.ShapeDtypeStruct((clusters, parts, rows, width), jnp.bfloat16)
    spec = pl.BlockSpec((1, parts, rows, width), lambda a: (a, 0, 0, 0))
    return pl.pallas_call(
        functools.partial(block_kernel, base, near_count, scale),
        grid=(clusters,),
        in_specs=[
            pl.BlockSpec(memory_space=pltpu.SMEM),
            pl.BlockSpec((1, slot_count, slots.shape[2]), lambda a: (a + base, 0, 0)),
            pl.BlockSpec(
                tuple(pl.Element(size) for size in (window, mark_count, depth)),
                lambda a: (base, 0, 0),
                pipeline_mode=pl.Buffered(1),
            ),
        ],
        out_specs=[spec, spec],
        out_shape=[shape, shape],
        compiler_params=pltpu.CompilerParams(vmem_limit_bytes=48 * 2**20),
        cost_estimate=pl.CostEstimate(
            flops=2**20,
            bytes_accessed=2**20,
            transcendentals=0,
        ),
    )(spots, slots, marks)


def on_device(compounds, targets, cluster_lists, landmarks, neighbours):
    lmk_count = lax.axis_size("lmk")
    cmp_count = lax.axis_size("cmp")
    my_lmk = lax.axis_index("lmk")
    my_cmp = lax.axis_index("cmp")
    owned, mark_count, width = landmarks.shape
    rim = owned // 2
    near_count = neighbours.shape[1]
    cluster_count = neighbours.shape[0]
    cap = cluster_lists.shape[1] * (2 * compounds.shape[0] // cluster_count)
    scale = 0.75 * math.sqrt(width)
    first = my_lmk * owned

    rows = jnp.concatenate([normalize(compounds), targets], axis=1)
    count, lanes = rows.shape
    picks = cluster_lists.shape[1]
    per_pick = -(-count // lanes)
    listed = jnp.pad(cluster_lists.T.astype(jnp.bfloat16), ((0, 0), (0, per_pick * lanes - count)))
    listed = listed.reshape(picks * per_pick, lanes)
    listed = jnp.pad(listed, ((0, -(picks * per_pick) % 16), (0, 0)))
    all_rows = lax.all_gather(jnp.concatenate([rows, listed], axis=0), "lmk")
    all_lists = all_rows[:, count : count + picks * per_pick].reshape(lmk_count, picks, -1)
    all_lists = all_lists[:, :, :count].astype(jnp.int32)

    forward = [(i, (i + 1) % lmk_count) for i in range(lmk_count)]
    backward = [(target, source) for source, target in forward]
    unit_marks = normalize(landmarks)
    portion = mark_count // cmp_count
    quarter = lax.dynamic_slice_in_dim(unit_marks, my_cmp * portion, portion, 1)
    low = lax.ppermute(quarter[owned - rim :], "lmk", forward)
    high = lax.ppermute(quarter[:rim], "lmk", backward)
    rims = jnp.concatenate([low, high], axis=0)
    edges = jnp.zeros((2 * rim, cmp_count, portion, width), jnp.bfloat16)
    for turn in range(cmp_count):
        swap = [(i, i ^ turn) for i in range(cmp_count)]
        piece = lax.ppermute(rims, "cmp", swap) if turn else rims
        edges = lax.dynamic_update_slice_in_dim(
            edges, piece[:, None], jnp.bitwise_xor(my_cmp, turn), 1
        )
    edges = edges.reshape(2 * rim, mark_count, width)
    extended = jnp.concatenate([edges[:rim], unit_marks, edges[rim:]], axis=0)
    lift = jnp.where(
        jnp.arange(owned + 2 * rim)[:, None, None] == jnp.arange(FLAG_LANES)[None, None, :],
        LIFT,
        0.0,
    ).astype(jnp.bfloat16)
    lift = jnp.broadcast_to(lift, (owned + 2 * rim, mark_count, FLAG_LANES))
    extended = jnp.concatenate([extended, lift], axis=2)

    near = lax.dynamic_slice_in_dim(neighbours, first, owned, 0)
    spots = jnp.mod(near - first + rim, cluster_count).reshape(-1)
    my_core = my_cmp % 2
    my_part = my_cmp // 2
    spots = jnp.concatenate([spots, my_core[None]]).astype(jnp.int32)

    slots = dispatch(
        jnp.asarray(first, jnp.int32)[None], all_lists, all_rows, owned, cap, cluster_count
    )
    slots = slots.reshape(owned, lmk_count * cap, slots.shape[3])
    parts = cmp_count // 2
    cores = [(i, i ^ 1) for i in range(cmp_count)]
    each = owned // CHUNKS
    done = []
    held = []
    crossed = []

    def cross(sums):
        pieces = []
        for hop in range(1, parts):
            across = [(i, (i + 2 * hop) % cmp_count) for i in range(cmp_count)]
            pieces.append(lax.ppermute(sums[hop], "cmp", across))
        return pieces

    for chunk in range(CHUNKS):
        if chunk > 1:
            spots, *held[chunk - 2] = lax.optimization_barrier((spots, *held[chunk - 2]))
            crossed.append(cross(held[chunk - 2]))
        if chunk > 2:
            spots, *crossed[chunk - 3] = lax.optimization_barrier((spots, *crossed[chunk - 3]))
        keep, send = blocks(
            chunk * each, each, near_count, scale, parts, spots, slots, extended
        )
        got = lax.ppermute(send, "cmp", cores)
        sums = []
        for hop in range(parts):
            part = (my_part + hop) % parts
            mine = lax.dynamic_index_in_dim(keep, part, 1, keepdims=False).astype(jnp.float32)
            mine += lax.dynamic_index_in_dim(got, part, 1, keepdims=False).astype(jnp.float32)
            sums.append(mine.astype(jnp.bfloat16) if hop else mine)
        held.append(sums)
    crossed += [cross(sums) for sums in held[len(crossed) :]]
    for sums, arrived in zip(held, crossed):
        pieces = sums[0]
        for piece in arrived:
            pieces += piece.astype(jnp.float32)
        done.append(jnp.transpose(pieces, (1, 0, 2)))
    shard = jnp.concatenate(done, axis=1)
    normal_blocks = shard[:, :, : near_count * mark_count].reshape(
        shard.shape[0], owned, near_count, mark_count
    )
    right_sides = shard[:, :, near_count * mark_count :]
    return (normal_blocks, right_sides)


def solution(mesh):
    placed = (
        P(("cmp", "lmk"), None),
        P(("cmp", "lmk"), None),
        P(("cmp", "lmk"), None),
        P("lmk", None, None),
        P(),
    )
    return jax.shard_map(
        on_device,
        mesh=mesh,
        in_specs=placed,
        out_specs=(P("cmp", "lmk", None, None), P("cmp", "lmk", None)),
        check_vma=False,
    )
```
